256 devices in a mesh: gx: 2 (over y_hi), gy: 16 (over z, y_lo), gz: 8 (over x, core).
Axes of the slice: x: 4, y: 4 (y_hi: 2, y_lo: 2; y = y_hi * 2 + y_lo), z: 8, core: 2. Of those that a mesh axis runs over, the one named last changes fastest.
Arguments:
- velocity: float32 [6, 128, 256, 1024], P(None, 'gx', 'gy', 'gz'), may hold values from -70 to 70, as said below
- basis_old: float32 [128, 96], P('gx'), may hold values from -0.5 to 0.5
- basis_mid: float32 [256, 96], P('gy'), may hold values from -0.375 to 0.375
- basis_deep: float32 [1024, 48], P('gz'), may hold values from -0.1875 to 0.1875
Outputs:
- basis_new: float32 [128, 96], P('gx')
- core_block: float32 [96, 48, 6, 96], P('gy', 'gz')
The draws below stay inside these ranges and needn't reach their ends.
Inputs may be any that keep to these rules, and one draw needn't show every extreme that they name: A velocity field of order one with a few shared flow patterns.
All inputs are finite; a program needn't handle non-finite values.
Results may differ from the reference program's by a relative error of at most 0.0003.
Values sent between devices are 32-bit elements; how exact they have to be, the bound alone decides.
No kernel may reach another device: no remote copies, remote signals or barrier semaphores. Data moves between devices by JAX's collectives and lax.ppermute only.
A program may use at most 128 MiB of HBM per device.

```python
import jax
import jax.numpy as jnp
from jax import lax

K = 6
R1 = 96
R2 = 96
R3 = 48
NX = 128
NY = 256
NZ = 1024


def draw_velocity(key, part):
    key = jax.random.fold_in(key, 11)
    keys = jax.random.split(key, 5)
    low_scale, high_scale, amplitude = (0.7, 1.4, 0.15)
    noise = jax.random.truncated_normal(keys[0], -6.0, 6.0, (K, NX, NY, NZ), jnp.float32)
    row_scale = jnp.exp(jax.random.uniform(keys[1], (1, NX, 1, 1), jnp.float32, jnp.log(low_scale), jnp.log(high_scale)))
    factor_a = jax.random.truncated_normal(keys[2], -4.0, 4.0, (4, K, NX, 1, 1), jnp.float32)
    factor_b = jax.random.truncated_normal(keys[3], -4.0, 4.0, (4, 1, 1, NY, 1), jnp.float32)
    factor_c = jax.random.truncated_normal(keys[4], -4.0, 4.0, (4, 1, 1, 1, NZ), jnp.float32)
    total = noise * row_scale
    for pattern in range(4):
        total = total + amplitude * factor_a[pattern] * factor_b[pattern] * factor_c[pattern]
    return total


def block_scale(stream_key, dims, cuts, low, top_value):
    level, own = 1.0, jax.random.fold_in(stream_key, 6)
    for axis_at, shards_of in cuts:
        heights = jnp.exp(jax.random.uniform(jax.random.fold_in(own, axis_at), (shards_of,), jnp.float32, low / len(cuts), top_value / len(cuts)))
        level = level * jnp.repeat(heights, dims[axis_at] // shards_of).reshape([-1 if axis == axis_at else 1 for axis in range(len(dims))])
    return level


def bell_draw(rng, dims, spread, most, pieces=(), dtype=jnp.bfloat16):
    gain = block_scale(rng, dims, pieces, -0.22, 0.18) if pieces else 1.0
    result = jax.random.normal(rng, dims, jnp.float32) * spread * gain
    return jnp.minimum(jnp.maximum(result, -most), most).astype(dtype)


def setup_inputs(seed: int = 0) -> dict:
    streams_of = jax.random.split(jax.random.key(seed), 5)
    velocity = draw_velocity(jax.random.fold_in(streams_of[4], 71), 0)
    basis_old = bell_draw(streams_of[1], (NX, R1), NX ** -0.5, 0.5, ((0, 2),), jnp.float32)
    basis_mid = bell_draw(streams_of[2], (NY, R2), NY ** -0.5, 0.375, ((0, 16),), jnp.float32)
    basis_deep = bell_draw(streams_of[3], (NZ, R3), NZ ** -0.5, 0.1875, ((0, 8),), jnp.float32)
    return dict(velocity=velocity, basis_old=basis_old, basis_mid=basis_mid, basis_deep=basis_deep)


def reference(velocity, basis_old, basis_mid, basis_deep):
    high = lax.Precision.HIGHEST
    partial_three = jnp.einsum('kabc,cr->kabr', velocity, basis_deep, precision=high)
    projected = jnp.einsum('kabr,bq->qrka', partial_three, basis_mid, precision=high)
    mixing = jnp.einsum('qrka,aj->qrkj', projected, basis_old, precision=high)
    image = jnp.einsum('qrka,qrkj->aj', projected, mixing, precision=high)
    gram = jnp.dot(image.T, image, precision=high)
    lower = jnp.linalg.cholesky(gram)
    basis_new = lax.linalg.triangular_solve(lower, image, left_side=False, lower=True, transpose_a=True)
    core_block = jnp.einsum('aj,qrka->qrkj', basis_new, projected, precision=high)
    return (basis_new, core_block)
```

```python
import functools

import jax
import jax.numpy as jnp
from jax import lax
from jax.experimental import pallas as pl
from jax.experimental.pallas import tpu as pltpu
from jax.sharding import Mesh, PartitionSpec as P

HIGH = lax.Precision.HIGHEST
F32 = jnp.float32
K, R1, NX = 6, 96, 128
XS, CORES, ZS, YS = 4, 2, 8, 4
PAIRS = 36
SLOTS = 5
TILES = 8


def dot(a, b, ca, cb):
    return lax.dot_general(a, b, (((ca,), (cb,)), ((), ())), precision=HIGH, preferred_element_type=F32)


def project_deep(vel_ref, deep_ref, send_ref, keep_ref):
    k = pl.program_id(0)
    me = lax.axis_index("x") * CORES + lax.axis_index("core")
    rows = []
    for core in (1, 0):
        for x in range(XS):
            rows.append(deep_ref[me ^ (x * CORES + core), :, :])
    deep = jnp.concatenate(rows, axis=0)
    for i in range(8):
        cells = jnp.concatenate([vel_ref[0, :, 2 * i, :], vel_ref[0, :, 2 * i + 1, :]], axis=0)
        part = dot(deep, cells, 1, 1)
        send_ref[pl.ds(k * 8 + i, 24, stride=48), :] = part[:24]
        keep_ref[pl.ds(k * 8 + i, 24, stride=48), :] = part[24:]


def pack_depth(a_ref, b_ref, c_ref, d_ref, mid_ref, old_ref, out_ref):
    z = lax.axis_index("z")
    source = lax.broadcasted_iota(jnp.int32, (R1, 128), 0)
    lane = lax.broadcasted_iota(jnp.int32, (R1, 128), 1)
    yl, zz, t = lane >> 6, (lane >> 3) & 7, lane & 7
    pick = jnp.where((source == (zz * 2 + yl) * 6 + t) & (t < 6), 1.0, 0.0).astype(F32)
    even = dot(mid_ref[pl.ds(0, 8, stride=2), :], pick, 1, 0)
    odd = dot(mid_ref[pl.ds(1, 8, stride=2), :], pick, 1, 0)
    old = jnp.concatenate([old_ref[pl.ds(pl.multiple_of(z * 8, 8), 8), :], jnp.zeros((8, 32), F32)], axis=1)
    for dest in range(ZS):
        for slot in range(SLOTS):
            pair = dest * SLOTS + slot
            if pair < PAIRS:
                at = pl.ds(pair * 8, 8)
                out_ref[dest, slot] = (a_ref[at, :] + b_ref[at, :]) + (c_ref[at, :] + d_ref[at, :])
            else:
                out_ref[dest, slot] = jnp.zeros((8, 128), F32)
        out_ref[dest, 5] = even
        out_ref[dest, 6] = odd
        out_ref[dest, 7] = old


def project_mid(r0, r1, r2, r3, image_ref, share_ref, whole):
    me = lax.axis_index("yh") * 2 + lax.axis_index("yl")
    for rel, ref in enumerate((r0, r1, r2, r3)):
        whole[me ^ rel] = ref[...]
    mids = []
    for yl in range(2):
        for par in range(2):
            mids.append(whole[yl, :, 5 + par].reshape(64, 128))
    mid = jnp.concatenate(mids, axis=0)
    mid_t = mid.T
    old = jnp.concatenate([whole[yh * 2, :, 7].reshape(64, 128) for yh in range(2)], axis=0)
    low = lax.broadcasted_iota(jnp.int32, (64, 128), 1) < 64
    parts = []
    for slot in range(SLOTS):
        rows = []
        for yl in range(2):
            first = whole[yl, :, slot].reshape(64, 128)
            second = whole[2 + yl, :, slot].reshape(64, 128)
            rows.append(jnp.where(low, first, pltpu.roll(second, 64, 1)))
            rows.append(jnp.where(low, pltpu.roll(first, 64, 1), second))
        parts.append(dot(mid_t, jnp.concatenate(rows, axis=0), 1, 0))
    yl = lax.axis_index("yl")
    for slot in range(SLOTS):
        half = jnp.where(yl == 0, parts[slot][:64], parts[slot][64:])
        for z in range(ZS):
            share_ref[z, slot] = half[z * 8:(z + 1) * 8]
    stack = jnp.concatenate(parts, axis=0)
    square = dot(stack, stack, 0, 0)
    image_ref[...] = dot(old[:, :R1], square, 0, 0)


def finish(p_ref, q_ref, share_ref, basis_ref, core_ref, rows_ref, turn_ref):
    image_t = p_ref[...] + q_ref[...]
    gram = dot(image_t, image_t, 1, 1)
    gram = jnp.concatenate([gram, jnp.zeros((R1, 128 - R1), F32)], axis=1)
    both = [jnp.concatenate([gram[8 * p:8 * p + 8], image_t[8 * p:8 * p + 8]], axis=1) for p in range(12)]
    row = lax.broadcasted_iota(jnp.int32, (8, 256), 0)
    done = []
    for p in range(12):
        d = both[p]
        for j in range(8):
            at = 8 * p + j
            col = d[:, at:at + 1]
            inv = lax.rsqrt(col[j:j + 1, :])
            pivot = d[j:j + 1, :] * inv
            d = jnp.where(row > j, d - (col * inv) * pivot, jnp.where(row == j, pivot, d))
        done.append(d[:, 128:])
        if p < 11:
            change = dot(d[:, :128], d, 0, 0)
            for r in range(p + 1, 12):
                both[r] = both[r] - change[8 * r:8 * r + 8]
    basis_t = jnp.concatenate(done, axis=0)
    turn_ref[...] = basis_t.T
    yh = lax.axis_index("yh")
    basis_ref[...] = turn_ref[pl.ds(pl.multiple_of(yh * 64, 64), 64), :]
    for t in range(6):
        for r in range(6):
            rows_ref[pl.ds((t * 6 + r) * 8, 6), :] = share_ref[pl.ds(r * 48 + t, 6, stride=8), :]
            rows_ref[pl.ds((t * 6 + r) * 8 + 6, 2), :] = jnp.zeros((2, 128), F32)
    core = dot(rows_ref[...], basis_t, 1, 1)
    core_ref[...] = core.reshape(6, 6, 8, R1)[:, :, :6, :]


VMEM = pl.BlockSpec(memory_space=pltpu.VMEM)


def call(kernel, outs, *args, scratch=()):
    return pl.pallas_call(
        kernel,
        out_shape=[jax.ShapeDtypeStruct(s, F32) for s in outs],
        in_specs=[VMEM] * len(args),
        out_specs=[VMEM] * len(outs),
        scratch_shapes=[pltpu.VMEM(s, F32) for s in scratch],
        compiler_params=pltpu.CompilerParams(vmem_limit_bytes=32 * 2**20),
    )(*args)


def swap(value, axis, size, bit):
    return lax.ppermute(value, axis, [(i, i ^ bit) for i in range(size)])


def on_device(velocity, basis_old, basis_mid, basis_deep):
    deep = basis_deep.T.reshape(8, 6, 128)
    rows = XS * PAIRS * 8
    send, keep = pl.pallas_call(
        project_deep,
        grid=(K,),
        out_shape=[jax.ShapeDtypeStruct((rows, 128), F32)] * 2,
        in_specs=[
            pl.BlockSpec((1, 64, 16, 128), lambda k: (k, 0, 0, 0)),
            pl.BlockSpec((8, 6, 128), lambda k: (0, 0, 0)),
        ],
        out_specs=[pl.BlockSpec((rows, 128), lambda k: (0, 0))] * 2,
        compiler_params=pltpu.CompilerParams(vmem_limit_bytes=32 * 2**20),
    )(velocity, deep)
    got = swap(send, "core", CORES, 1)
    keep, got = (v.reshape(XS, PAIRS * 8, 128) for v in (keep, got))
    sums = [keep[m] + got[m] for m in range(XS)]
    others = [swap(sums[m], "x", XS, m) for m in (2, 1, 3)]
    (packed,) = call(pack_depth, [(ZS, TILES, 8, 128)], sums[0], others[1], others[0], others[2], basis_mid, basis_old)
    mine = lax.all_to_all(packed, "z", 0, 0, tiled=True)
    near = {m: swap(mine, ("yh", "yl"), YS, m) for m in (2, 1, 3)}
    image, share = call(
        project_mid,
        [(R1, NX), (ZS, SLOTS, 8, 128)],
        mine, near[1], near[2], near[3],
        scratch=[(YS, ZS, TILES, 8, 128)],
    )
    shares = lax.all_to_all(share, "z", 0, 0, tiled=True)
    for axis, size, bit in (("core", 2, 1), ("x", 4, 1), ("x", 4, 3), ("z", 8, 1), ("z", 8, 2)):
        image = image + swap(image, axis, size, bit)
    last = swap(image, "z", 8, 7)
    basis_new, core_block = call(
        finish,
        [(64, R1), (6, 6, 6, R1)],
        image, last, shares.reshape(ZS * SLOTS * 8, 128),
        scratch=[(288, 128), (NX, R1)],
    )
    return (basis_new, core_block)


def solution(mesh):
    parts = Mesh(mesh.devices.reshape(2, 8, 2, 4, 2), ("yh", "z", "yl", "x", "core"))
    placed = (P(None, "yh", ("z", "yl"), ("x", "core")), P("yh", None), P(("z", "yl"), None), P(("x", "core"), None))
    return jax.shard_map(
        on_device,
        mesh=parts,
        in_specs=placed,
        out_specs=(P("yh", None), P(("z", "yl"), ("x", "core"), None, None)),
        check_vma=False,
    )
```

```python
import jax
import jax.numpy as jnp
from jax import lax
from jax.experimental import pallas as pl
from jax.experimental.pallas import tpu as pltpu
from jax.sharding import Mesh, PartitionSpec as P

HIGH = lax.Precision.HIGHEST
F32, BF16 = jnp.float32, jnp.bfloat16
K, R1, NX = 6, 96, 128
XS, CORES, ZS, YS = 4, 2, 8, 4
PAIRS = 36
SLOTS = 5
TILES = 7
HALF = SLOTS * 48


def dot(a, b, ca, cb, precision=HIGH):
    return lax.dot_general(a, b, (((ca,), (cb,)), ((), ())), precision=precision, preferred_element_type=F32)


def halves(value):
    high = value.astype(BF16)
    return high, (value - high.astype(F32)).astype(BF16)


def project_deep(vel_ref, deep_ref, send_ref, keep_ref, cells_ref, sems):
    copies = [pltpu.make_async_copy(vel_ref.at[k], cells_ref.at[k], sems.at[k]) for k in range(K)]
    for copy in copies:
        copy.start()
    me = lax.axis_index("x") * CORES + lax.axis_index("core")
    rows = [deep_ref[me ^ (x * CORES + core)] for core in (1, 0) for x in range(XS)]
    high, low = halves(jnp.concatenate(rows, axis=0))
    deep = jnp.concatenate([jnp.concatenate([high, high], axis=1), jnp.concatenate([low, low], axis=1)], axis=0)
    for k in range(K):
        copies[k].wait()
        for i in range(0, 8, 2):
            cells = jnp.concatenate([cells_ref[k, :, b, :] for b in range(2 * i, 2 * i + 4)], axis=0)
            part = dot(deep, jnp.concatenate(halves(cells), axis=1), 1, 1, None)
            part = part[:48] + part[48:]
            for s in range(2):
                at = pl.ds(k * 8 + i + s, 24, stride=48)
                send_ref[at, :] = part[:24, s * 128:s * 128 + 128]
                keep_ref[at, :] = part[24:, s * 128:s * 128 + 128]


def pack_depth(a_ref, b_ref, c_ref, d_ref, mid_ref, out_ref):
    source = lax.broadcasted_iota(jnp.int32, (R1, 128), 0)
    lane = lax.broadcasted_iota(jnp.int32, (R1, 128), 1)
    yl = jnp.where(lane >= 48, 1, 0)
    at = lane - 48 * yl
    z = ((at.astype(F32) + 0.5) * (1.0 / 6.0)).astype(jnp.int32)
    pick = jnp.where((source == at + 6 * z + 6 * yl) & (lane < R1), 1.0, 0.0).astype(F32)
    even = dot(mid_ref[pl.ds(0, 8, stride=2), :], pick, 1, 0)
    odd = dot(mid_ref[pl.ds(1, 8, stride=2), :], pick, 1, 0)
    for dest in range(ZS):
        for slot in range(SLOTS):
            pair = dest * SLOTS + slot
            if pair < PAIRS:
                at = pl.ds(pair * 8, 8)
                out_ref[dest, slot] = (a_ref[at, :] + b_ref[at, :]) + (c_ref[at, :] + d_ref[at, :])
            else:
                out_ref[dest, slot] = jnp.zeros((8, 128), F32)
        out_ref[dest, 5] = even
        out_ref[dest, 6] = odd


def project_mid(got_ref, old_ref, part_ref, more_ref):
    mid = jnp.concatenate([got_ref[:, 5 + par].reshape(64, 128).T[:R1] for par in range(2)], axis=0)
    cells = jnp.concatenate([got_ref[:, slot].reshape(64, 128) for slot in range(SLOTS)], axis=1)
    both = dot(mid, cells, 1, 0)
    low = lax.broadcasted_iota(jnp.int32, (48, 128), 1) < 64
    for slot in range(SLOTS):
        at = slice(slot * 128, slot * 128 + 128)
        e0, e1, o0, o1 = (both[r * 48:r * 48 + 48, at] for r in range(4))
        first = e0 + pltpu.roll(o0, 64, 1)
        second = pltpu.roll(e1, 64, 1) + o1
        out = jnp.where(low, first, second)
        part_ref[slot * 48:slot * 48 + 48, :] = out
        more_ref[slot * 48:slot * 48 + 48, :] = out
    more_ref[HALF:HALF + 64, :] = jnp.concatenate([old_ref[...], jnp.zeros((64, 128 - R1), F32)], axis=1)


def form_image(own_ref, r1, r2, r3, old_ref, image_ref, share_ref):
    yh, yl = lax.axis_index("yh"), lax.axis_index("yl")
    near = own_ref[...] + r1[...]
    far = r2[:HALF, :] + r3[...]
    h0 = jnp.where(yh == 0, near, far)
    h1 = jnp.where(yh == 0, far, near)
    low = lax.broadcasted_iota(jnp.int32, (HALF, 128), 1) < 64
    p0 = jnp.where(low, h0, pltpu.roll(h1, 64, 1))
    p1 = jnp.where(low, pltpu.roll(h0, 64, 1), h1)
    mine = jnp.where(yl == 0, p0, p1)
    for slot in range(SLOTS):
        for z in range(ZS):
            share_ref[z, slot, 0:6, :] = mine[slot * 48 + z * 6:slot * 48 + z * 6 + 6]
    stack = jnp.concatenate([p0, p1], axis=0)
    square = dot(stack, stack, 0, 0)
    other = r2[HALF:HALF + 64, :R1]
    own = old_ref[...]
    old = jnp.concatenate([jnp.where(yh == 0, own, other), jnp.where(yh == 0, other, own)], axis=0)
    image_ref[...] = dot(old, square, 0, 0)


def solve(gram, image_t):
    size = 32
    count = R1 // size
    gram = jnp.concatenate([gram, jnp.zeros((R1, 128 - R1), F32)], axis=1)
    left = [gram[size * p:size * p + size] for p in range(count)]
    right = [image_t[size * p:size * p + size] for p in range(count)]
    row = lax.broadcasted_iota(jnp.int32, (size, 128), 0)
    done = []
    for p in range(count):
        a, x = left[p], right[p]
        columns = [jnp.broadcast_to(a[:, size * p + j:size * p + j + 1], (size, 128)) for j in range(size)]
        for j in range(size):
            inv = lax.rsqrt(columns[j][j:j + 1, :])
            m = columns[j] * inv
            for i in range(j + 1, size):
                columns[i] = columns[i] - m * m[i:i + 1, :]
            pa, px = a[j:j + 1, :] * inv, x[j:j + 1, :] * inv
            a = jnp.where(row > j, a - m * pa, jnp.where(row == j, pa, a))
            x = jnp.where(row > j, x - m * px, jnp.where(row == j, px, x))
        done.append(x)
        if p < count - 1:
            change = dot(a.T[size * (p + 1):R1], jnp.concatenate([a, x], axis=1), 1, 0)
            for r in range(p + 1, count):
                at = size * (r - p - 1)
                left[r] = left[r] - change[at:at + size, :128]
                right[r] = right[r] - change[at:at + size, 128:]
    return jnp.concatenate(done, axis=0)


def finish(p_ref, q_ref, share_ref, basis_ref, core_ref, rows_ref, turn_ref):
    image_t = p_ref[...] + q_ref[...]
    basis_t = solve(dot(image_t, image_t, 1, 1), image_t)
    turn_ref[...] = basis_t.T
    yh = lax.axis_index("yh")
    basis_ref[...] = turn_ref[pl.ds(pl.multiple_of(yh * 64, 64), 64), :]
    for t in range(6):
        for r in range(6):
            rows_ref[pl.ds((t * 6 + r) * 8, 6), :] = share_ref[pl.ds(r * 48 + t, 6, stride=8), :]
            rows_ref[pl.ds((t * 6 + r) * 8 + 6, 2), :] = jnp.zeros((2, 128), F32)
    core = dot(rows_ref[...], basis_t, 1, 1)
    core_ref[...] = core.reshape(6, 6, 8, R1)[:, :, :6, :]


VMEM = pl.BlockSpec(memory_space=pltpu.VMEM)


def call(kernel, outs, *args, scratch=()):
    return pl.pallas_call(
        kernel,
        out_shape=[jax.ShapeDtypeStruct(s, F32) for s in outs],
        in_specs=[VMEM] * len(args),
        out_specs=[VMEM] * len(outs),
        scratch_shapes=[pltpu.VMEM(s, F32) for s in scratch],
        compiler_params=pltpu.CompilerParams(vmem_limit_bytes=32 * 2**20),
    )(*args)


def swap(value, axis, size, bit):
    return lax.ppermute(value, axis, [(i, i ^ bit) for i in range(size)])


def on_device(velocity, basis_old, basis_mid, basis_deep):
    deep = basis_deep.T.reshape(8, 6, 128)
    rows = XS * PAIRS * 8
    send, keep = pl.pallas_call(
        project_deep,
        out_shape=[jax.ShapeDtypeStruct((rows, 128), F32)] * 2,
        in_specs=[pl.BlockSpec(memory_space=pltpu.HBM), VMEM],
        out_specs=[VMEM] * 2,
        scratch_shapes=[pltpu.VMEM((K, 64, 16, 128), F32), pltpu.SemaphoreType.DMA((K,))],
        compiler_params=pltpu.CompilerParams(vmem_limit_bytes=32 * 2**20),
    )(velocity, deep)
    got = swap(send, "core", CORES, 1)
    keep, got = (v.reshape(XS, PAIRS * 8, 128) for v in (keep, got))
    sums = [keep[m] + got[m] for m in range(XS)]
    others = {m: swap(sums[m], "x", XS, m) for m in (3, 1, 2)}
    (packed,) = call(pack_depth, [(ZS, TILES, 8, 128)], sums[0], others[1], others[2], others[3], basis_mid)
    mine = lax.all_to_all(packed, "z", 0, 0, tiled=True)
    part, more = call(project_mid, [(HALF, 128), (HALF + 64, 128)], mine, basis_old)
    near = {m: swap(more if m == 2 else part, ("yh", "yl"), YS, m) for m in (3, 1, 2)}
    image, share = call(
        form_image, [(R1, NX), (ZS, SLOTS, 8, 128)], part, near[1], near[2], near[3], basis_old
    )
    shares = lax.all_to_all(share, "z", 0, 0, tiled=True)
    for axis, size, bit in (("core", 2, 1), ("x", 4, 1), ("x", 4, 3), ("z", 8, 1), ("z", 8, 2)):
        image = image + swap(image, axis, size, bit)
    last = swap(image, "z", 8, 7)
    basis_new, core_block = call(
        finish,
        [(64, R1), (6, 6, 6, R1)],
        image, last, shares.reshape(ZS * SLOTS * 8, 128),
        scratch=[(288, 128), (NX, R1)],
    )
    return (basis_new, core_block)


def solution(mesh):
    parts = Mesh(mesh.devices.reshape(2, 8, 2, 4, 2), ("yh", "z", "yl", "x", "core"))
    placed = (P(None, "yh", ("z", "yl"), ("x", "core")), P("yh", None), P(("z", "yl"), None), P(("x", "core"), None))
    return jax.shard_map(
        on_device,
        mesh=parts,
        in_specs=placed,
        out_specs=(P("yh", None), P(("z", "yl"), ("x", "core"), None, None)),
        check_vma=False,
    )
```

```python
import jax
import jax.numpy as jnp
from jax import lax
from jax.experimental import pallas as pl
from jax.experimental.pallas import tpu as pltpu
from jax.sharding import Mesh, PartitionSpec as P

HIGH = lax.Precision.HIGHEST
F32, BF16 = jnp.float32, jnp.bfloat16
K, R1, NX = 6, 96, 128
XS, CORES, ZS, YS = 4, 2, 8, 4
KP, PP = 3, 18
PAIRS = 36
SLOTS = 5
TILES = 7
G1, G2, G3 = 1, 2, 7
HALF = SLOTS * 48


def dot(a, b, ca, cb, precision=HIGH):
    return lax.dot_general(a, b, (((ca,), (cb,)), ((), ())), precision=precision, preferred_element_type=F32)


def halves(value):
    high = value.astype(BF16)
    return high, (value - high.astype(F32)).astype(BF16)


def project_cells(k, cells_ref, deep, send_ref, keep_ref):
    for i in range(0, 8, 2):
        cells = jnp.concatenate([cells_ref[k, :, b, :] for b in range(2 * i, 2 * i + 4)], axis=0)
        out = dot(deep, jnp.concatenate(halves(cells), axis=1), 1, 1, None)
        out = out[:48] + out[48:]
        for s in range(2):
            at = pl.ds(k * 8 + i + s, 24, stride=KP * 8)
            send_ref[at, :] = out[:24, s * 128:s * 128 + 128]
            keep_ref[at, :] = out[24:, s * 128:s * 128 + 128]


def ranks(deep_ref):
    me = lax.axis_index("x") * CORES + lax.axis_index("core")
    rows = [deep_ref[pl.ds((me ^ (x * CORES + core)) * 6, 6), :] for core in (1, 0) for x in range(XS)]
    high, low = halves(jnp.concatenate(rows, axis=0))
    return jnp.concatenate([jnp.concatenate([high, high], axis=1), jnp.concatenate([low, low], axis=1)], axis=0)


def project_first(vel_ref, deep_ref, send_ref, keep_ref, next_ref, cells_ref, sems):
    copies = [pltpu.make_async_copy(vel_ref.at[k], cells_ref.at[k], sems.at[k]) for k in range(KP)]
    copies.append(pltpu.make_async_copy(vel_ref.at[pl.ds(KP, K - KP)], next_ref, sems.at[KP]))
    for copy in copies:
        copy.start()
    deep = ranks(deep_ref)
    for k in range(KP):
        copies[k].wait()
        project_cells(k, cells_ref, deep, send_ref, keep_ref)
    copies[KP].wait()


def project_rest(cells_ref, deep_ref, send_ref, keep_ref):
    deep = ranks(deep_ref)
    for k in range(KP):
        project_cells(k, cells_ref, deep, send_ref, keep_ref)


def pack_depth(a0, b0, c0, d0, a1, b1, c1, d1, mid_ref, out_ref):
    source = lax.broadcasted_iota(jnp.int32, (R1, 128), 0)
    lane = lax.broadcasted_iota(jnp.int32, (R1, 128), 1)
    yl = jnp.where(lane >= 48, 1, 0)
    at = lane - 48 * yl
    z = ((at.astype(F32) + 0.5) * (1.0 / 6.0)).astype(jnp.int32)
    pick = jnp.where((source == at + 6 * z + 6 * yl) & (lane < R1), 1.0, 0.0).astype(F32)
    even = dot(mid_ref[pl.ds(0, 8, stride=2), :], pick, 1, 0)
    odd = dot(mid_ref[pl.ds(1, 8, stride=2), :], pick, 1, 0)
    for dest in range(ZS):
        for slot in range(SLOTS):
            pair = dest * SLOTS + slot
            if pair < PAIRS:
                a, b, c, d = (a0, b0, c0, d0) if pair < PP else (a1, b1, c1, d1)
                at = pl.ds(pair % PP * 8, 8)
                out_ref[dest, slot] = (a[at, :] + b[at, :]) + (c[at, :] + d[at, :])
            else:
                out_ref[dest, slot] = jnp.zeros((8, 128), F32)
        out_ref[dest, 5] = even
        out_ref[dest, 6] = odd


def project_mid(got_ref, old_ref, part_ref, more_ref):
    mid = jnp.concatenate([got_ref[:, 5 + par].reshape(64, 128).T[:R1] for par in range(2)], axis=0)
    cells = jnp.concatenate([got_ref[:, slot].reshape(64, 128) for slot in range(SLOTS)], axis=1)
    both = dot(mid, cells, 1, 0)
    low = lax.broadcasted_iota(jnp.int32, (48, 128), 1) < 64
    for slot in range(SLOTS):
        at = slice(slot * 128, slot * 128 + 128)
        e0, e1, o0, o1 = (both[r * 48:r * 48 + 48, at] for r in range(4))
        first = e0 + pltpu.roll(o0, 64, 1)
        second = pltpu.roll(e1, 64, 1) + o1
        out = jnp.where(low, first, second)
        part_ref[slot * 48:slot * 48 + 48, :] = out
        more_ref[slot * 48:slot * 48 + 48, :] = out
    more_ref[HALF:HALF + 64, :] = jnp.concatenate([old_ref[...], jnp.zeros((64, 128 - R1), F32)], axis=1)


def form_image(own_ref, r1, r2, r3, old_ref, image_ref, a1_ref, a2_ref, a3_ref, a0_ref, mine_ref):
    yh, yl, z = lax.axis_index("yh"), lax.axis_index("yl"), lax.axis_index("z")
    near = own_ref[...] + r1[...]
    far = r2[:HALF, :] + r3[...]
    h0 = jnp.where(yh == 0, near, far)
    h1 = jnp.where(yh == 0, far, near)
    low = lax.broadcasted_iota(jnp.int32, (HALF, 128), 1) < 64
    p0 = jnp.where(low, h0, pltpu.roll(h1, 64, 1))
    p1 = jnp.where(low, pltpu.roll(h0, 64, 1), h1)
    stack = jnp.concatenate([p0, p1], axis=0)
    square = dot(stack, stack, 0, 0)
    other = r2[HALF:HALF + 64, :R1]
    own = old_ref[...]
    old = jnp.concatenate([jnp.where(yh == 0, own, other), jnp.where(yh == 0, other, own)], axis=0)
    image_ref[...] = dot(old, square, 0, 0)
    mine_ref[...] = jnp.where(yl == 0, p0, p1)
    plan = (
        (a1_ref, (G1 ^ G2, G1 ^ G2 ^ G3, G1 ^ G3, G1)),
        (a2_ref, (G2, G2 ^ G3)),
        (a3_ref, (G3,)),
        (a0_ref, (0,)),
    )
    for ref, places in plan:
        for i, m in enumerate(places):
            for slot in range(SLOTS):
                ref[i, slot, 0:6, :] = mine_ref[pl.ds(slot * 48 + (z ^ m) * 6, 6), :]


def solve(gram, image_t):
    size = 32
    count = R1 // size
    gram = jnp.concatenate([gram, jnp.zeros((R1, 128 - R1), F32)], axis=1)
    left = [gram[size * p:size * p + size] for p in range(count)]
    right = [image_t[size * p:size * p + size] for p in range(count)]
    row = lax.broadcasted_iota(jnp.int32, (size, 128), 0)
    done = []
    for p in range(count):
        a, x = left[p], right[p]
        columns = [jnp.broadcast_to(a[:, size * p + j:size * p + j + 1], (size, 128)) for j in range(size)]
        for j in range(size):
            inv = lax.rsqrt(columns[j][j:j + 1, :])
            m = columns[j] * inv
            for i in range(j + 1, size):
                columns[i] = columns[i] - m * m[i:i + 1, :]
            pa, px = a[j:j + 1, :] * inv, x[j:j + 1, :] * inv
            a = jnp.where(row > j, a - m * pa, jnp.where(row == j, pa, a))
            x = jnp.where(row > j, x - m * px, jnp.where(row == j, px, x))
        done.append(x)
        if p < count - 1:
            change = dot(a.T[size * (p + 1):R1], jnp.concatenate([a, x], axis=1), 1, 0)
            for r in range(p + 1, count):
                at = size * (r - p - 1)
                left[r] = left[r] - change[at:at + size, :128]
                right[r] = right[r] - change[at:at + size, 128:]
    return jnp.concatenate(done, axis=0)


def finish(p_ref, q_ref, a0_ref, r1_ref, r2_ref, r3_ref, basis_ref, core_ref, rows_ref, turn_ref):
    yh, z = lax.axis_index("yh"), lax.axis_index("z")
    held = [(0, a0_ref, 0), (G1, r1_ref, 3), (G2, r2_ref, 0), (G1 ^ G2, r2_ref, 2)]
    held += [(G3 ^ m, r3_ref, i) for i, m in enumerate((0, G1, G2, G1 ^ G2))]
    for m, ref, i in held:
        for slot in range(SLOTS):
            pair = (z ^ m) * SLOTS + slot
            at = jnp.where(pair < PAIRS, pair % PP // KP * 8 + pair // PP * KP + pair % KP, 7)
            rows_ref[pl.ds(at, 6, stride=48), :] = ref[i, slot, 0:6, :]
    image_t = p_ref[...] + q_ref[...]
    basis_t = solve(dot(image_t, image_t, 1, 1), image_t)
    turn_ref[...] = basis_t.T
    basis_ref[...] = turn_ref[pl.ds(pl.multiple_of(yh * 64, 64), 64), :]
    core = dot(rows_ref[...], basis_t, 1, 1)
    core_ref[...] = core.reshape(6, 6, 8, R1)[:, :, :6, :]


VMEM = pl.BlockSpec(memory_space=pltpu.VMEM)


def call(kernel, outs, *args, scratch=()):
    return pl.pallas_call(
        kernel,
        out_shape=[jax.ShapeDtypeStruct(s, F32) for s in outs],
        in_specs=[VMEM] * len(args),
        out_specs=[VMEM] * len(outs),
        scratch_shapes=[pltpu.VMEM(s, F32) for s in scratch],
        compiler_params=pltpu.CompilerParams(vmem_limit_bytes=32 * 2**20),
    )(*args)


def swap(value, axis, size, bit):
    return lax.ppermute(value, axis, [(i, i ^ bit) for i in range(size)])


def across(value, a, b):
    axes = ("z", "x", "core")
    one, two, both = (
        lax.ppermute(value, axes, [(i, i ^ m) for i in range(ZS * XS * CORES)]) for m in (a, b, a ^ b)
    )
    return (value + one) + (two + both)


def shift(value, by):
    return lax.ppermute(value, "z", [(i, (i - by) % ZS) for i in range(ZS)])


def on_device(velocity, basis_old, basis_mid, basis_deep):
    deep = basis_deep.T
    parts = [(XS * PP * 8, 128)] * 2
    send, keep, cells = pl.pallas_call(
        project_first,
        out_shape=[jax.ShapeDtypeStruct(s, F32) for s in (*parts, (K - KP, 64, 16, 128))],
        in_specs=[pl.BlockSpec(memory_space=pltpu.HBM), VMEM],
        out_specs=[VMEM] * 3,
        scratch_shapes=[pltpu.VMEM((KP, 64, 16, 128), F32), pltpu.SemaphoreType.DMA((KP + 1,))],
        compiler_params=pltpu.CompilerParams(vmem_limit_bytes=51 * 2**20),
    )(velocity, deep)
    sums = []
    for part in range(2):
        if part:
            send, keep = call(project_rest, parts, cells, deep)
        got = swap(send, "core", CORES, 1)
        keep, got = (v.reshape(XS, PP * 8, 128) for v in (keep, got))
        own = [keep[m] + got[m] for m in range(XS)]
        others = {m: swap(own[m], "x", XS, m) for m in (3, 1, 2)}
        sums += [own[0], others[1], others[2], others[3]]
    (packed,) = call(pack_depth, [(ZS, TILES, 8, 128)], *sums, basis_mid)
    mine = lax.all_to_all(packed, "z", 0, 0, tiled=True)
    part, more = call(project_mid, [(HALF, 128), (HALF + 64, 128)], mine, basis_old)
    near = {m: swap(more if m == 2 else part, ("yh", "yl"), YS, m) for m in (3, 1, 2)}
    block = (SLOTS, 8, 128)
    image, a1, a2, a3, a0 = call(
        form_image,
        [(R1, NX), (4, *block), (2, *block), (1, *block), (1, *block)],
        part, near[1], near[2], near[3], basis_old,
        scratch=[(HALF, 128)],
    )
    b1 = swap(a1, "z", ZS, G1)
    b2 = swap(jnp.concatenate([a2, b1[:2]]), "z", ZS, G2)
    b3 = swap(jnp.concatenate([a3, b1[2:3], b2[1:2], b2[3:4]]), "z", ZS, G3)
    image = across(image, 1, 2)
    image = across(image, 6, 8)
    image = image + swap(image, "z", 8, 2)
    last = swap(image, "z", ZS, 7)
    basis_new, core_block = call(
        finish,
        [(64, R1), (6, 6, 6, R1)],
        image, last, a0, b1, b2, b3,
        scratch=[(288, 128), (NX, R1)],
    )
    return (basis_new, core_block)


def solution(mesh):
    parts = Mesh(mesh.devices.reshape(2, 8, 2, 4, 2), ("yh", "z", "yl", "x", "core"))
    placed = (P(None, "yh", ("z", "yl"), ("x", "core")), P("yh", None), P(("z", "yl"), None), P(("x", "core"), None))
    return jax.shard_map(
        on_device,
        mesh=parts,
        in_specs=placed,
        out_specs=(P("yh", None), P(("z", "yl"), ("x", "core"), None, None)),
        check_vma=False,
    )
```

```python
import jax
import jax.numpy as jnp
from jax import lax
from jax.experimental import pallas as pl
from jax.experimental.pallas import tpu as pltpu
from jax.sharding import Mesh, PartitionSpec as P

HIGH = lax.Precision.HIGHEST
F32, BF16 = jnp.float32, jnp.bfloat16
K, R1, NX = 6, 96, 128
XS, CORES, ZS, YS = 4, 2, 8, 4
KP, PP = 3, 18
PAIRS = 36
SLOTS = 5
TILES = 7
G1, G2, G3 = 1, 2, 6
HALF = SLOTS * 48


def dot(a, b, ca, cb, precision=HIGH):
    return lax.dot_general(a, b, (((ca,), (cb,)), ((), ())), precision=precision, preferred_element_type=F32)


def halves(value):
    high = value.astype(BF16)
    return high, (value - high.astype(F32)).astype(BF16)


def project_cells(k, cells_ref, deep, send_ref, keep_ref):
    for i in range(0, 8, 2):
        cells = jnp.concatenate([cells_ref[k, :, b, :] for b in range(2 * i, 2 * i + 4)], axis=0)
        out = dot(deep, jnp.concatenate(halves(cells), axis=1), 1, 1, None)
        out = out[:48] + out[48:]
        for s in range(2):
            at = pl.ds(k * 8 + i + s, 24, stride=KP * 8)
            send_ref[at, :] = out[:24, s * 128:s * 128 + 128]
            keep_ref[at, :] = out[24:, s * 128:s * 128 + 128]


def ranks(deep_ref):
    me = lax.axis_index("x") * CORES + lax.axis_index("core")
    rows = [deep_ref[pl.ds((me ^ (x * CORES + core)) * 6, 6), :] for core in (1, 0) for x in range(XS)]
    high, low = halves(jnp.concatenate(rows, axis=0))
    return jnp.concatenate([jnp.concatenate([high, high], axis=1), jnp.concatenate([low, low], axis=1)], axis=0)


def fetch(vel_ref, cells_ref, sem):
    copy = pltpu.make_async_copy(vel_ref.at[pl.ds(0, KP)], cells_ref, sem)
    copy.start()
    copy.wait()


def project_first(cells_ref, vel_ref, deep_ref, send_ref, keep_ref, next_ref, sem):
    copy = pltpu.make_async_copy(vel_ref.at[pl.ds(KP, K - KP)], next_ref, sem)
    copy.start()
    deep = ranks(deep_ref)
    for k in range(KP):
        project_cells(k, cells_ref, deep, send_ref, keep_ref)
    copy.wait()


def project_rest(cells_ref, deep_ref, send_ref, keep_ref):
    deep = ranks(deep_ref)
    for k in range(KP):
        project_cells(k, cells_ref, deep, send_ref, keep_ref)


def pack_depth(a0, b0, c0, d0, a1, b1, c1, d1, mid_ref, out_ref):
    source = lax.broadcasted_iota(jnp.int32, (R1, 128), 0)
    lane = lax.broadcasted_iota(jnp.int32, (R1, 128), 1)
    yl = jnp.where(lane >= 48, 1, 0)
    at = lane - 48 * yl
    z = ((at.astype(F32) + 0.5) * (1.0 / 6.0)).astype(jnp.int32)
    pick = jnp.where((source == at + 6 * z + 6 * yl) & (lane < R1), 1.0, 0.0).astype(F32)
    even = dot(mid_ref[pl.ds(0, 8, stride=2), :], pick, 1, 0)
    odd = dot(mid_ref[pl.ds(1, 8, stride=2), :], pick, 1, 0)
    for dest in range(ZS):
        for slot in range(SLOTS):
            pair = dest * SLOTS + slot
            if pair < PAIRS:
                a, b, c, d = (a0, b0, c0, d0) if pair < PP else (a1, b1, c1, d1)
                at = pl.ds(pair % PP * 8, 8)
                out_ref[dest, slot] = (a[at, :] + b[at, :]) + (c[at, :] + d[at, :])
            else:
                out_ref[dest, slot] = jnp.zeros((8, 128), F32)
        out_ref[dest, 5] = even
        out_ref[dest, 6] = odd


def project_mid(got_ref, old_ref, part_ref, more_ref):
    mid = jnp.concatenate([got_ref[:, 5 + par].reshape(64, 128).T[:R1] for par in range(2)], axis=0)
    cells = jnp.concatenate([got_ref[:, slot].reshape(64, 128) for slot in range(SLOTS)], axis=1)
    mid_high, mid_low = halves(mid)
    left = jnp.concatenate(
        [jnp.concatenate([mid_high, mid_high], axis=1), jnp.concatenate([mid_low, mid_low], axis=1)], axis=0
    )
    both = dot(left, jnp.concatenate(halves(cells), axis=0), 1, 0, None)
    both = both[:2 * R1] + both[2 * R1:]
    low = lax.broadcasted_iota(jnp.int32, (48, 128), 1) < 64
    for slot in range(SLOTS):
        at = slice(slot * 128, slot * 128 + 128)
        e0, e1, o0, o1 = (both[r * 48:r * 48 + 48, at] for r in range(4))
        first = e0 + pltpu.roll(o0, 64, 1)
        second = pltpu.roll(e1, 64, 1) + o1
        out = jnp.where(low, first, second)
        part_ref[slot * 48:slot * 48 + 48, :] = out
        more_ref[slot * 48:slot * 48 + 48, :] = out
    more_ref[HALF:HALF + 64, :] = jnp.concatenate([old_ref[...], jnp.zeros((64, 128 - R1), F32)], axis=1)


def form_image(own_ref, r1, r2, r3, old_ref, image_ref, a1_ref, a2_ref, a3_ref, a0_ref, mine_ref):
    yh, yl, z = lax.axis_index("yh"), lax.axis_index("yl"), lax.axis_index("z")
    near = own_ref[...] + r1[...]
    far = r2[:HALF, :] + r3[...]
    h0 = jnp.where(yh == 0, near, far)
    h1 = jnp.where(yh == 0, far, near)
    low = lax.broadcasted_iota(jnp.int32, (HALF, 128), 1) < 64
    p0 = jnp.where(low, h0, pltpu.roll(h1, 64, 1))
    p1 = jnp.where(low, pltpu.roll(h0, 64, 1), h1)
    high, low = halves(jnp.concatenate([p0, p1], axis=0))
    left = jnp.concatenate([high, low], axis=0)
    right = jnp.concatenate([left, jnp.concatenate([low, high], axis=0)], axis=1)
    square = dot(left, right, 0, 0, None)
    square = square[:, :NX] + square[:, NX:]
    other = r2[HALF:HALF + 64, :R1]
    own = old_ref[...]
    old = jnp.concatenate([jnp.where(yh == 0, own, other), jnp.where(yh == 0, other, own)], axis=0)
    image_ref[...] = dot(old, square, 0, 0)
    mine_ref[...] = jnp.where(yl == 0, p0, p1)
    plan = (
        (a1_ref, (G1 ^ G2, G1 ^ G2 ^ G3, G1 ^ G3, G1)),
        (a2_ref, (G2, G2 ^ G3)),
        (a3_ref, (G3,)),
        (a0_ref, (0,)),
    )
    for ref, places in plan:
        for i, m in enumerate(places):
            for slot in range(SLOTS):
                ref[i, slot, 0:6, :] = mine_ref[pl.ds(slot * 48 + (z ^ m) * 6, 6), :]


def solve(gram, image_t):
    size = 32
    count = R1 // size
    gram = jnp.concatenate([gram, jnp.zeros((R1, 128 - R1), F32)], axis=1)
    left = [gram[size * p:size * p + size] for p in range(count)]
    right = [image_t[size * p:size * p + size] for p in range(count)]
    row = lax.broadcasted_iota(jnp.int32, (size, 128), 0)
    done = []
    for p in range(count):
        a, x = left[p], right[p]
        columns = [jnp.broadcast_to(a[:, size * p + j:size * p + j + 1], (size, 128)) for j in range(size)]
        for j in range(size):
            inv = lax.rsqrt(columns[j][j:j + 1, :])
            m = columns[j] * inv
            for i in range(j + 1, size):
                columns[i] = columns[i] - m * m[i:i + 1, :]
            pa, px = a[j:j + 1, :] * inv, x[j:j + 1, :] * inv
            a = jnp.where(row > j, a - m * pa, jnp.where(row == j, pa, a))
            x = jnp.where(row > j, x - m * px, jnp.where(row == j, px, x))
        done.append(x)
        if p < count - 1:
            change = dot(a.T[size * (p + 1):R1], jnp.concatenate([a, x], axis=1), 1, 0)
            for r in range(p + 1, count):
                at = size * (r - p - 1)
                left[r] = left[r] - change[at:at + size, :128]
                right[r] = right[r] - change[at:at + size, 128:]
    return jnp.concatenate(done, axis=0)


def gather_rows(a0_ref, r1_ref, r2_ref, r3_ref, rows_ref):
    z = lax.axis_index("z")
    held = [(0, a0_ref, 0), (G1, r1_ref, 3), (G2, r2_ref, 0), (G1 ^ G2, r2_ref, 2)]
    held += [(G3 ^ m, r3_ref, i) for i, m in enumerate((0, G1, G2, G1 ^ G2))]
    for m, ref, i in held:
        for slot in range(SLOTS):
            pair = (z ^ m) * SLOTS + slot
            at = jnp.where(pair < PAIRS, pair % PP // KP * 8 + pair // PP * KP + pair % KP, 7)
            rows_ref[pl.ds(at, 6, stride=48), :] = ref[i, slot, 0:6, :]


def finish(p_ref, q_ref, rows_ref, basis_ref, core_ref, turn_ref):
    yh = lax.axis_index("yh")
    image_t = p_ref[...] + q_ref[...]
    basis_t = solve(dot(image_t, image_t, 1, 1), image_t)
    turn_ref[...] = basis_t.T
    basis_ref[...] = turn_ref[pl.ds(pl.multiple_of(yh * 64, 64), 64), :]
    high, low = halves(jnp.concatenate([basis_t, jnp.zeros((128 - R1, NX), F32)], axis=0))
    right = jnp.concatenate(
        [jnp.concatenate([high, high], axis=1), jnp.concatenate([low, low], axis=1)], axis=0
    )
    core = dot(jnp.concatenate(halves(rows_ref[...]), axis=1), right, 1, 1, None)
    core = core[:, :R1] + core[:, 128:128 + R1]
    core_ref[...] = core.reshape(6, 6, 8, R1)[:, :, :6, :]


VMEM = pl.BlockSpec(memory_space=pltpu.VMEM)


def call(kernel, outs, *args, scratch=()):
    return pl.pallas_call(
        kernel,
        out_shape=[jax.ShapeDtypeStruct(s, F32) for s in outs],
        in_specs=[VMEM] * len(args),
        out_specs=[VMEM] * len(outs),
        scratch_shapes=[pltpu.VMEM(s, F32) for s in scratch],
        compiler_params=pltpu.CompilerParams(vmem_limit_bytes=32 * 2**20),
    )(*args)


def swap(value, axis, size, bit):
    return lax.ppermute(value, axis, [(i, i ^ bit) for i in range(size)])


def across(value, a, b):
    axes = ("z", "x", "core")
    one, two, both = (
        lax.ppermute(value, axes, [(i, i ^ m) for i in range(ZS * XS * CORES)]) for m in (a, b, a ^ b)
    )
    return (value + one) + (two + both)


def shift(value, by):
    return lax.ppermute(value, "z", [(i, (i - by) % ZS) for i in range(ZS)])


def on_device(velocity, basis_old, basis_mid, basis_deep):
    deep = basis_deep.T
    parts = [(XS * PP * 8, 128)] * 2
    block = (KP, 64, 16, 128)
    limit = pltpu.CompilerParams(vmem_limit_bytes=50 * 2**20)
    cells = pl.pallas_call(
        fetch,
        out_shape=jax.ShapeDtypeStruct(block, F32),
        in_specs=[pl.BlockSpec(memory_space=pltpu.HBM)],
        out_specs=VMEM,
        scratch_shapes=[pltpu.SemaphoreType.DMA],
        compiler_params=limit,
    )(velocity)
    send, keep, cells = pl.pallas_call(
        project_first,
        out_shape=[jax.ShapeDtypeStruct(s, F32) for s in (*parts, block)],
        in_specs=[VMEM, pl.BlockSpec(memory_space=pltpu.HBM), VMEM],
        out_specs=[VMEM] * 3,
        scratch_shapes=[pltpu.SemaphoreType.DMA],
        compiler_params=limit,
    )(cells, velocity, deep)
    sums = []
    for part in range(2):
        if part:
            send, keep = call(project_rest, parts, cells, deep)
        got = swap(send, "core", CORES, 1)
        keep, got = (v.reshape(XS, PP * 8, 128) for v in (keep, got))
        own = [keep[m] + got[m] for m in range(XS)]
        others = {m: swap(own[m], "x", XS, m) for m in (3, 1, 2)}
        sums += [own[0], others[1], others[2], others[3]]
    (packed,) = call(pack_depth, [(ZS, TILES, 8, 128)], *sums, basis_mid)
    mine = lax.all_to_all(packed, "z", 0, 0, tiled=True)
    part, more = call(project_mid, [(HALF, 128), (HALF + 64, 128)], mine, basis_old)
    near = {m: swap(more if m == 2 else part, ("yh", "yl"), YS, m) for m in (3, 1, 2)}
    block = (SLOTS, 8, 128)
    image, a1, a2, a3, a0 = call(
        form_image,
        [(R1, NX), (4, *block), (2, *block), (1, *block), (1, *block)],
        part, near[1], near[2], near[3], basis_old,
        scratch=[(HALF, 128)],
    )
    b1 = swap(a1, "z", ZS, G1)
    b2 = swap(jnp.concatenate([a2, b1[:2]]), "z", ZS, G2)
    b3 = swap(jnp.concatenate([a3, b1[2:3], b2[1:2], b2[3:4]]), "z", ZS, G3)
    image = across(image, 1, 8)
    image = across(image, 2, 6)
    image = image + swap(image, "z", ZS, 6)
    last = swap(image, "z", ZS, 2)
    (rows,) = call(gather_rows, [(288, 128)], a0, b1, b2, b3)
    basis_new, core_block = call(
        finish,
        [(64, R1), (6, 6, 6, R1)],
        image, last, rows,
        scratch=[(NX, R1)],
    )
    return (basis_new, core_block)


def solution(mesh):
    parts = Mesh(mesh.devices.reshape(2, 8, 2, 4, 2), ("yh", "z", "yl", "x", "core"))
    placed = (P(None, "yh", ("z", "yl"), ("x", "core")), P("yh", None), P(("z", "yl"), None), P(("x", "core"), None))
    return jax.shard_map(
        on_device,
        mesh=parts,
        in_specs=placed,
        out_specs=(P("yh", None), P(("z", "yl"), ("x", "core"), None, None)),
        check_vma=False,
    )
```

```python
import jax
import jax.numpy as jnp
from jax import lax
from jax.experimental import pallas as pl
from jax.experimental.pallas import tpu as pltpu
from jax.sharding import Mesh, PartitionSpec as P

HIGH = lax.Precision.HIGHEST
F32, BF16 = jnp.float32, jnp.bfloat16
K, R1, NX = 6, 96, 128
XS, CORES, ZS, YS = 4, 2, 8, 4
KP, PP = 3, 18
PAIRS = 36
SLOTS = 5
TILES = 7
G1, G2, G3 = 1, 2, 6
HALF = SLOTS * 48


def dot(a, b, ca, cb, precision=HIGH):
    return lax.dot_general(a, b, (((ca,), (cb,)), ((), ())), precision=precision, preferred_element_type=F32)


def halves(value):
    high = value.astype(BF16)
    return high, (value - high.astype(F32)).astype(BF16)


def project_cells(k, cells_ref, deep, send_ref, keep_ref):
    for i in range(0, 8, 2):
        cells = jnp.concatenate([cells_ref[k, :, b, :] for b in range(2 * i, 2 * i + 4)], axis=0)
        out = dot(deep, jnp.concatenate(halves(cells), axis=1), 1, 1, None)
        out = out[:48] + out[48:]
        for s in range(2):
            at = pl.ds(k * 8 + i + s, 24, stride=KP * 8)
            send_ref[at, :] = out[:24, s * 128:s * 128 + 128]
            keep_ref[at, :] = out[24:, s * 128:s * 128 + 128]


def ranks(deep_ref):
    me = lax.axis_index("x") * CORES + lax.axis_index("core")
    rows = [deep_ref[pl.ds((me ^ (x * CORES + core)) * 6, 6), :] for core in (1, 0) for x in range(XS)]
    high, low = halves(jnp.concatenate(rows, axis=0))
    return jnp.concatenate([jnp.concatenate([high, high], axis=1), jnp.concatenate([low, low], axis=1)], axis=0)


def fetch(vel_ref, cells_ref, sem):
    copy = pltpu.make_async_copy(vel_ref.at[pl.ds(0, KP)], cells_ref, sem)
    copy.start()
    copy.wait()


def project_first(cells_ref, vel_ref, deep_ref, send_ref, keep_ref, next_ref, sem):
    copy = pltpu.make_async_copy(vel_ref.at[pl.ds(KP, K - KP)], next_ref, sem)
    copy.start()
    deep = ranks(deep_ref)
    for k in range(KP):
        project_cells(k, cells_ref, deep, send_ref, keep_ref)
    copy.wait()


def project_rest(cells_ref, deep_ref, send_ref, keep_ref):
    deep = ranks(deep_ref)
    for k in range(KP):
        project_cells(k, cells_ref, deep, send_ref, keep_ref)


def pack_depth(a0, b0, c0, d0, a1, b1, c1, d1, mid_ref, out_ref):
    source = lax.broadcasted_iota(jnp.int32, (R1, 128), 0)
    lane = lax.broadcasted_iota(jnp.int32, (R1, 128), 1)
    yl = jnp.where(lane >= 48, 1, 0)
    at = lane - 48 * yl
    z = ((at.astype(F32) + 0.5) * (1.0 / 6.0)).astype(jnp.int32)
    pick = jnp.where((source == at + 6 * z + 6 * yl) & (lane < R1), 1.0, 0.0).astype(F32)
    even = dot(mid_ref[pl.ds(0, 8, stride=2), :], pick, 1, 0)
    odd = dot(mid_ref[pl.ds(1, 8, stride=2), :], pick, 1, 0)
    for dest in range(ZS):
        for slot in range(SLOTS):
            pair = dest * SLOTS + slot
            if pair < PAIRS:
                a, b, c, d = (a0, b0, c0, d0) if pair < PP else (a1, b1, c1, d1)
                at = pl.ds(pair % PP * 8, 8)
                out_ref[dest, slot] = (a[at, :] + b[at, :]) + (c[at, :] + d[at, :])
            else:
                out_ref[dest, slot] = jnp.zeros((8, 128), F32)
        out_ref[dest, 5] = even
        out_ref[dest, 6] = odd


def project_mid(got_ref, old_ref, part_ref, more_ref):
    mid = jnp.concatenate([got_ref[:, 5 + par].reshape(64, 128).T[:R1] for par in range(2)], axis=0)
    cells = jnp.concatenate([got_ref[:, slot].reshape(64, 128) for slot in range(SLOTS)], axis=1)
    mid_high, mid_low = halves(mid)
    left = jnp.concatenate(
        [jnp.concatenate([mid_high, mid_high], axis=1), jnp.concatenate([mid_low, mid_low], axis=1)], axis=0
    )
    both = dot(left, jnp.concatenate(halves(cells), axis=0), 1, 0, None)
    both = both[:2 * R1] + both[2 * R1:]
    low = lax.broadcasted_iota(jnp.int32, (48, 128), 1) < 64
    for slot in range(SLOTS):
        at = slice(slot * 128, slot * 128 + 128)
        e0, e1, o0, o1 = (both[r * 48:r * 48 + 48, at] for r in range(4))
        first = e0 + pltpu.roll(o0, 64, 1)
        second = pltpu.roll(e1, 64, 1) + o1
        out = jnp.where(low, first, second)
        part_ref[slot * 48:slot * 48 + 48, :] = out
        more_ref[slot * 48:slot * 48 + 48, :] = out
    more_ref[HALF:HALF + 64, :] = jnp.concatenate([old_ref[...], jnp.zeros((64, 128 - R1), F32)], axis=1)


def form_image(own_ref, r1, r2, r3, old_ref, image_ref, a1_ref, a2_ref, a3_ref, a0_ref, mine_ref):
    yh, yl, z = lax.axis_index("yh"), lax.axis_index("yl"), lax.axis_index("z")
    near = own_ref[...] + r1[...]
    far = r2[...] + r3[:HALF, :]
    h0 = jnp.where(yh == 0, near, far)
    h1 = jnp.where(yh == 0, far, near)
    low = lax.broadcasted_iota(jnp.int32, (HALF, 128), 1) < 64
    p0 = jnp.where(low, h0, pltpu.roll(h1, 64, 1))
    p1 = jnp.where(low, pltpu.roll(h0, 64, 1), h1)
    high, low = halves(jnp.concatenate([p0, p1], axis=0))
    left = jnp.concatenate([high, low], axis=0)
    right = jnp.concatenate([left, jnp.concatenate([low, high], axis=0)], axis=1)
    square = dot(left, right, 0, 0, None)
    square = square[:, :NX] + square[:, NX:]
    other = r3[HALF:HALF + 64, :R1]
    own = old_ref[...]
    old = jnp.concatenate([jnp.where(yh == 0, own, other), jnp.where(yh == 0, other, own)], axis=0)
    image_ref[...] = dot(old, square, 0, 0)
    mine_ref[...] = jnp.where(yl == 0, p0, p1)
    plan = (
        (a1_ref, (G1 ^ G2, G1 ^ G2 ^ G3, G1 ^ G3, G1)),
        (a2_ref, (G2, G2 ^ G3)),
        (a3_ref, (G3,)),
        (a0_ref, (0,)),
    )
    for ref, places in plan:
        for i, m in enumerate(places):
            for slot in range(SLOTS):
                ref[i, slot, 0:6, :] = mine_ref[pl.ds(slot * 48 + (z ^ m) * 6, 6), :]


def solve(gram, image_t):
    size = 32
    count = R1 // size
    gram = jnp.concatenate([gram, jnp.zeros((R1, 128 - R1), F32)], axis=1)
    left = [gram[size * p:size * p + size] for p in range(count)]
    right = [image_t[size * p:size * p + size] for p in range(count)]
    row = lax.broadcasted_iota(jnp.int32, (size, 128), 0)
    done = []
    for p in range(count):
        a, x = left[p], right[p]
        columns = [jnp.broadcast_to(a[:, size * p + j:size * p + j + 1], (size, 128)) for j in range(size)]
        for j in range(size):
            inv = lax.rsqrt(columns[j][j:j + 1, :])
            m = columns[j] * inv
            for i in range(j + 1, size):
                columns[i] = columns[i] - m * m[i:i + 1, :]
            pa, px = a[j:j + 1, :] * inv, x[j:j + 1, :] * inv
            a = jnp.where(row > j, a - m * pa, jnp.where(row == j, pa, a))
            x = jnp.where(row > j, x - m * px, jnp.where(row == j, px, x))
        done.append(x)
        if p < count - 1:
            change = dot(a.T[size * (p + 1):R1], jnp.concatenate([a, x], axis=1), 1, 0)
            for r in range(p + 1, count):
                at = size * (r - p - 1)
                left[r] = left[r] - change[at:at + size, :128]
                right[r] = right[r] - change[at:at + size, 128:]
    return jnp.concatenate(done, axis=0)


def gather_rows(a0_ref, r1_ref, r2_ref, r3_ref, rows_ref):
    z = lax.axis_index("z")
    held = [(0, a0_ref, 0), (G1, r1_ref, 3), (G2, r2_ref, 0), (G1 ^ G2, r2_ref, 2)]
    held += [(G3 ^ m, r3_ref, i) for i, m in enumerate((0, G1, G2, G1 ^ G2))]
    for m, ref, i in held:
        for slot in range(SLOTS):
            pair = (z ^ m) * SLOTS + slot
            at = jnp.where(pair < PAIRS, pair % PP // KP * 8 + pair // PP * KP + pair % KP, 7)
            rows_ref[pl.ds(at, 6, stride=48), :] = ref[i, slot, 0:6, :]


def finish(p_ref, q_ref, rows_ref, basis_ref, core_ref, turn_ref):
    yh = lax.axis_index("yh")
    image_t = p_ref[...] + q_ref[...]
    basis_t = solve(dot(image_t, image_t, 1, 1), image_t)
    turn_ref[...] = basis_t.T
    basis_ref[...] = turn_ref[pl.ds(pl.multiple_of(yh * 64, 64), 64), :]
    high, low = halves(jnp.concatenate([basis_t, jnp.zeros((128 - R1, NX), F32)], axis=0))
    right = jnp.concatenate(
        [jnp.concatenate([high, high], axis=1), jnp.concatenate([low, low], axis=1)], axis=0
    )
    core = dot(jnp.concatenate(halves(rows_ref[...]), axis=1), right, 1, 1, None)
    core = core[:, :R1] + core[:, 128:128 + R1]
    core_ref[...] = core.reshape(6, 6, 8, R1)[:, :, :6, :]


VMEM = pl.BlockSpec(memory_space=pltpu.VMEM)


def call(kernel, outs, *args, scratch=()):
    return pl.pallas_call(
        kernel,
        out_shape=[jax.ShapeDtypeStruct(s, F32) for s in outs],
        in_specs=[VMEM] * len(args),
        out_specs=[VMEM] * len(outs),
        scratch_shapes=[pltpu.VMEM(s, F32) for s in scratch],
        compiler_params=pltpu.CompilerParams(vmem_limit_bytes=32 * 2**20),
    )(*args)


def swap(value, axis, size, bit):
    return lax.ppermute(value, axis, [(i, i ^ bit) for i in range(size)])


def across(value, a, b):
    axes = ("z", "x", "core")
    one, two, both = (
        lax.ppermute(value, axes, [(i, i ^ m) for i in range(ZS * XS * CORES)]) for m in (a, b, a ^ b)
    )
    return (value + one) + (two + both)


def shift(value, by):
    return lax.ppermute(value, "z", [(i, (i - by) % ZS) for i in range(ZS)])


def on_device(velocity, basis_old, basis_mid, basis_deep):
    deep = basis_deep.T
    parts = [(XS * PP * 8, 128)] * 2
    block = (KP, 64, 16, 128)
    limit = pltpu.CompilerParams(vmem_limit_bytes=50 * 2**20)
    cells = pl.pallas_call(
        fetch,
        out_shape=jax.ShapeDtypeStruct(block, F32),
        in_specs=[pl.BlockSpec(memory_space=pltpu.HBM)],
        out_specs=VMEM,
        scratch_shapes=[pltpu.SemaphoreType.DMA],
        compiler_params=limit,
    )(velocity)
    send, keep, cells = pl.pallas_call(
        project_first,
        out_shape=[jax.ShapeDtypeStruct(s, F32) for s in (*parts, block)],
        in_specs=[VMEM, pl.BlockSpec(memory_space=pltpu.HBM), VMEM],
        out_specs=[VMEM] * 3,
        scratch_shapes=[pltpu.SemaphoreType.DMA],
        compiler_params=limit,
    )(cells, velocity, deep)
    sums = []
    for part in range(2):
        if part:
            send, keep = call(project_rest, parts, cells, deep)
        got = swap(send, "core", CORES, 1)
        keep, got = (v.reshape(XS, PP * 8, 128) for v in (keep, got))
        own = [keep[m] + got[m] for m in range(XS)]
        others = {m: swap(own[m], "x", XS, m) for m in (3, 1, 2)}
        sums += [own[0], others[1], others[2], others[3]]
    (packed,) = call(pack_depth, [(ZS, TILES, 8, 128)], *sums, basis_mid)
    mine = lax.all_to_all(packed, "z", 0, 0, tiled=True)
    part, more = call(project_mid, [(HALF, 128), (HALF + 64, 128)], mine, basis_old)
    near = {m: swap(more if m == 3 else part, ("yh", "yl"), YS, m) for m in (3, 1, 2)}
    block = (SLOTS, 8, 128)
    image, a1, a2, a3, a0 = call(
        form_image,
        [(R1, NX), (4, *block), (2, *block), (1, *block), (1, *block)],
        part, near[1], near[2], near[3], basis_old,
        scratch=[(HALF, 128)],
    )
    b1 = swap(a1, "z", ZS, G1)
    b2 = swap(jnp.concatenate([a2, b1[:2]]), "z", ZS, G2)
    b3 = swap(jnp.concatenate([a3, b1[2:3], b2[1:2], b2[3:4]]), "z", ZS, G3)
    image = across(image, 1, 8)
    image = across(image, 2, 6)
    image = image + swap(image, "z", ZS, 6)
    last = swap(image, "z", ZS, 2)
    (rows,) = call(gather_rows, [(288, 128)], a0, b1, b2, b3)
    basis_new, core_block = call(
        finish,
        [(64, R1), (6, 6, 6, R1)],
        image, last, rows,
        scratch=[(NX, R1)],
    )
    return (basis_new, core_block)


def solution(mesh):
    parts = Mesh(mesh.devices.reshape(2, 8, 2, 4, 2), ("yh", "z", "yl", "x", "core"))
    placed = (P(None, "yh", ("z", "yl"), ("x", "core")), P("yh", None), P(("z", "yl"), None), P(("x", "core"), None))
    return jax.shard_map(
        on_device,
        mesh=parts,
        in_specs=placed,
        out_specs=(P("yh", None), P(("z", "yl"), ("x", "core"), None, None)),
        check_vma=False,
    )
```
